32 devices in a mesh: groups: 2 (over y), adapt: 16 (over z, x, core).
Axes of the slice: x: 2, y: 2, z: 4, core: 2. Of those that a mesh axis runs over, the one named last changes fastest.
Arguments:
- hidden: bfloat16 [2048, 8192], P(('groups', 'adapt')), parts along dimension 0, may hold values from -6 to 6
- frozen_query: bfloat16 [2048, 8192], P(('groups', 'adapt')), parts along dimension 0, may hold values from -30 to 30
- keys: bfloat16 [32, 1088, 1024], P(('groups', 'adapt')), parts along dimension 0, may hold values from -24 to 24
- values: bfloat16 [32, 1088, 1024], P(('groups', 'adapt')), parts along dimension 0, may hold values from -6 to 6
- cache_length: int32 [32], P(('groups', 'adapt')), parts along dimension 0, may hold values from 1 to 1024, 8192 in all
- adapter_index: int32 [2048, 2], P(('groups', 'adapt')), parts along dimension 0, may hold values from 0 to 127, all different within a row; in each aligned block of 64 rows (0 to 63, 64 to 127, ...) at most 2 rows name the same one
- adapter_down_weight: bfloat16 [256, 32, 8192], P(('groups', 'adapt')), parts along dimension 0, may hold values from -0.0625 to 0.0625
- adapter_up_weight: bfloat16 [256, 32, 8192], P(('groups', 'adapt')), parts along dimension 0, may hold values from -1 to 1
Outputs:
- context: bfloat16 [2048, 2, 8192], P(('groups', 'adapt')), parts along dimension 0
The draws below stay inside these ranges and needn't reach their ends.
There are 2 independent parts, one for each index of `groups`. The reference program is written for one: setup_inputs(seed, part) draws one part's arguments, and reference() takes and returns one part's arrays. A program takes and returns all parts, laid end to end along the dimension named above; each array names one. Nothing has to cross between parts.
Inputs may be any that keep to these rules, and one draw needn't show every extreme that they name: `adapter_index`: among the 64 tokens of one device (with 2 ids each), no adapter is named more than 2 times, a bound that some block reaches; the 2 ids of a token differ. `cache_length`: within each part the live slots of the 16 prompts sum to 8192.
All inputs are finite; a program needn't handle non-finite values. No bound on the sum of `cache_length` on one device may be relied on, other than what follows from the above.
Results may differ from the reference program's by a relative error of at most 0.0083.
Values may be sent and summed in bfloat16 or wider, within the bound.
A program may use at most 192 MiB of HBM per device.

```python
import math
import jax
import jax.numpy as jnp
import numpy as np
from jax import lax

MODEL_DIMENSION = 8192
HEADS = 64
HEAD = 128
KV_HEADS = 8
ADAPTER_RANK = 32
ADAPTER_COUNT = 128
CAP = 2
TOP = 2
TOK_DEV = 64
CTX = 1024
KV_W = 1024
KEYS = 1088
PROMPTS = 16
TOKENS = 1024


def key_rows(key):
    base = jnp.clip(jax.random.normal(key, (PROMPTS, CTX + TOK_DEV, KV_HEADS, HEAD), jnp.float32), -6.0, 6.0)
    return base


def draw_keys(key, part):
    rows = key_rows(key)
    return rows.reshape(PROMPTS, CTX + TOK_DEV, KV_HEADS * HEAD).astype(jnp.bfloat16)


def draw_frozen_query(key, part):
    key = jax.random.fold_in(key, 5)
    own = jnp.clip(jax.random.normal(key, (TOKENS, HEADS, HEAD), jnp.float32), -6.0, 6.0)
    return own.reshape(TOKENS, HEADS * HEAD).astype(jnp.bfloat16)


def steps_of(rng, shape, shards, least, largest):
    factor_of = 1.0
    for dim, parts in shards:
        draws = jax.random.uniform(jax.random.fold_in(jax.random.fold_in(rng, 6), dim), (parts,), jnp.float32, least / len(shards), largest / len(shards))
        factor_of = factor_of * jnp.repeat(jnp.exp(draws), shape[dim] // parts).reshape((-1,) + (1,) * (len(shape) - 1 - dim))
    return factor_of


def split_up(number_of, total, limit, lean):
    portions = [(1 << 20) // math.isqrt(rank ** lean) + 1 for rank in range(2, number_of + 1)]
    spare, holding = total - limit - (number_of - 1), [1] * (number_of - 1)
    while spare > 0:
        movable = [i for i in range(number_of - 1) if holding[i] < limit]
        whole, budget = sum([portions[i] for i in movable]), spare
        for i in movable:
            extra = min(limit - holding[i], max(1, budget * portions[i] // whole), spare)
            holding[i] = holding[i] + extra
            spare = spare - extra
    return np.array([limit] + holding)


def uneven(own_key, amount, total, most, skew):
    if amount == 2:
        one = jax.random.randint(own_key, (), max(1, total - most), min(most, total - 1) + 1)
        return jnp.stack([one, total - one])
    sizes = jnp.asarray(split_up(amount, total, most, skew), jnp.int32)
    couples = (amount - 1) // 2
    source_of, taker = sizes[1:1 + 2 * couples:2], sizes[2:2 + 2 * couples:2]
    slack = jnp.minimum(source_of - 1, most - taker)
    shifted = jax.random.randint(jax.random.fold_in(own_key, 1), (couples,), 0, 1 << 20) % (slack + 1)
    sizes = sizes.at[1:1 + 2 * couples:2].set(source_of - shifted).at[2:2 + 2 * couples:2].set(taker + shifted)
    return sizes[jax.random.permutation(jax.random.fold_in(own_key, 2), amount)]


def assign_block(rng, own, number, rows, number_of, top, bound, slope):
    ranking = jax.random.permutation(rng, number_of)
    packed, usual = shares(number_of, rows * top, bound, slope, True), shares(number_of, rows * top, bound, slope, False)
    places = jnp.arange(number_of)

    def named(sizes, turn):
        used = int((sizes > 0).sum())
        fixed = max(1, used // 4)
        passed = fixed + (places - fixed + turn * (used - fixed)) % max(1, number_of - fixed)
        return jnp.zeros((number_of,), jnp.int32).at[ranking[jnp.where(places < fixed, places, passed)]].set(jnp.asarray(sizes, jnp.int32))

    sizes = jnp.where(number % 4 == 0, named(packed, number // 4), named(usual, number - number // 4 - 1))
    mixed = jax.random.permutation(jax.random.fold_in(own, 3), number_of)
    source_of, sink = mixed[0:number_of // 2 * 2:2], mixed[1:number_of // 2 * 2:2]
    room = jnp.minimum(sizes[source_of] - 1, bound - sizes[sink]) // 2
    room = jnp.where((source_of == ranking[0]) | (sink == ranking[0]) | (sizes[sink] == 0), 0, jnp.maximum(room, 0))
    passed = jax.random.randint(jax.random.fold_in(own, 4), (number_of // 2,), 0, 1 << 20) % (room + 1)
    sizes = sizes.at[source_of].add(-passed).at[sink].add(passed)
    labels = jnp.searchsorted(jnp.cumsum(sizes), jnp.arange(rows * top), side="right").astype(jnp.int32)
    table = labels.reshape(top, rows).T
    table = table[jax.random.permutation(jax.random.fold_in(own, 1), rows)]
    turn = jax.random.randint(jax.random.fold_in(own, 2), (rows, 1), 0, top)
    return jnp.take_along_axis(table, (jnp.arange(top)[None, :] + turn) % top, axis=1)


def shares(amount, total, reach, lean, full):
    loads = [(1 << 20) // math.isqrt(rank ** lean) + 1 for rank in range(1, amount + 1)]
    largest = reach if full else min(reach, max(-(-total // amount), total * loads[0] // sum(loads)))
    least = 1 if total - largest >= amount - 1 else 0
    holding, rest = [largest] + [least] * (amount - 1), total - largest - least * (amount - 1)
    while rest > 0:
        candidates = [i for i in range(1, amount) if holding[i] < largest] or [i for i in range(1, amount) if holding[i] < reach]
        whole, budget = sum([loads[i] for i in candidates]), rest
        for i in candidates:
            addition = min(reach - holding[i], max(1, budget * loads[i] // whole), rest)
            holding[i] = holding[i] + addition
            rest = rest - addition
    return np.array(holding)


def gaussian(key, extent, width, most, cuts=(), kind=jnp.bfloat16):
    array = width * jax.random.normal(key, extent, jnp.float32)
    if cuts:
        array = array * steps_of(key, extent, cuts, -0.22, 0.18)
    return jnp.clip(array, -most, most).astype(kind)


def setup_inputs(seed: int = 0, part: int = 0) -> dict:
    seeds = jax.random.split(jax.random.key(seed), 9)
    part_keys = jax.random.split(jax.random.fold_in(seeds[8], part), 9)
    hidden = gaussian(part_keys[0], (TOKENS, MODEL_DIMENSION), 1.0, 6.0, ((0, 16),))
    frozen_query = draw_frozen_query(jax.random.fold_in(jax.random.fold_in(seeds[8], part), 71), part)
    keys = draw_keys(jax.random.fold_in(jax.random.fold_in(seeds[8], part), 71), part)
    values = gaussian(part_keys[3], (PROMPTS, KEYS, KV_W), 1.0, 6.0, ((0, 16),))
    cache_length = uneven(part_keys[4], PROMPTS, PROMPTS * CTX // 2, CTX, 2).astype(jnp.int32)
    adapter_index_keys = jax.random.split(jax.random.fold_in(part_keys[5], 1), TOKENS // TOK_DEV)
    adapter_index_turns = jax.random.permutation(jax.random.fold_in(part_keys[5], 3), TOKENS // TOK_DEV)
    adapter_index = jax.vmap(lambda own, number: assign_block(jax.random.fold_in(part_keys[5], 2), own, number, TOK_DEV, ADAPTER_COUNT, TOP, CAP, 2))(adapter_index_keys, adapter_index_turns).reshape((TOKENS, TOP))
    adapter_down_weight = gaussian(part_keys[6], (ADAPTER_COUNT, ADAPTER_RANK, MODEL_DIMENSION), MODEL_DIMENSION ** -0.5, 0.0625, ((0, 16),))
    adapter_up_weight = gaussian(part_keys[7], (ADAPTER_COUNT, ADAPTER_RANK, MODEL_DIMENSION), ADAPTER_RANK ** -0.5, 1.0, ((0, 16),))
    return dict(hidden=hidden, frozen_query=frozen_query, keys=keys, values=values, cache_length=cache_length, adapter_index=adapter_index, adapter_down_weight=adapter_down_weight, adapter_up_weight=adapter_up_weight)


ADAPTER_SCALE = 0.5

def attend(adapted_query_rows, key_block, value_block, cached):
    tok_rows, per_token, model_width = adapted_query_rows.shape
    key_total, kv_width = key_block.shape
    kv_heads = kv_width // HEAD
    group_size = model_width // kv_width
    split_query = adapted_query_rows.reshape(tok_rows, per_token, kv_heads, group_size, HEAD).astype(jnp.float32)
    split_keys = key_block.reshape(key_total, kv_heads, HEAD).astype(jnp.float32)
    split_values = value_block.reshape(key_total, kv_heads, HEAD).astype(jnp.float32)
    scores = jnp.einsum('tagqe,jge->tagqj', split_query, split_keys) * (1.0 / math.sqrt(HEAD))
    key_index = lax.broadcasted_iota(jnp.int32, (tok_rows, key_total), 1)
    tok_index = lax.broadcasted_iota(jnp.int32, (tok_rows, key_total), 0)
    history = key_total - tok_rows
    visible = (key_index >= history - cached) & (key_index <= history + tok_index)
    visible = visible[:, None, None, None, :]
    scores = jnp.where(visible, scores, -1e+30)
    row_peak = lax.optimization_barrier(jnp.max(scores, axis=-1, keepdims=True))
    raised = jnp.where(visible, jnp.exp(scores - row_peak), 0.0)
    weights = (raised / lax.optimization_barrier(jnp.sum(raised, axis=-1, keepdims=True))).astype(jnp.bfloat16)
    mixed_rows = jnp.einsum('tagqj,jge->tagqe', weights.astype(jnp.float32), split_values)
    return mixed_rows.reshape(tok_rows, per_token, model_width).astype(jnp.bfloat16)

def reference(hidden, frozen_query, keys, values, cache_length, adapter_index, adapter_down_weight, adapter_up_weight):
    prompt_total = keys.shape[0]
    hidden_blocks = hidden.reshape(prompt_total, TOK_DEV, MODEL_DIMENSION)
    query_blocks = frozen_query.reshape(prompt_total, TOK_DEV, MODEL_DIMENSION)
    id_blocks = adapter_index.reshape(prompt_total, TOK_DEV, TOP)

    def one_prompt(items):
        block_hidden, query_block_rows, block_keys, block_values, cached, block_adapter_index = items
        down_weight_rows = adapter_down_weight[block_adapter_index].astype(jnp.float32)
        reduced_rows = jnp.einsum('te,tkre->tkr', block_hidden.astype(jnp.float32), down_weight_rows).astype(jnp.bfloat16)
        up_weight_rows = adapter_up_weight[block_adapter_index].astype(jnp.float32)
        lowrank_update = jnp.einsum('tkr,tkre->tke', reduced_rows.astype(jnp.float32), up_weight_rows).astype(jnp.bfloat16)
        adapted_query_rows = (query_block_rows[:, None, :].astype(jnp.float32) + ADAPTER_SCALE * lowrank_update.astype(jnp.float32)).astype(jnp.bfloat16)
        return attend(adapted_query_rows, block_keys, block_values, cached)
    result = lax.map(one_prompt, (hidden_blocks, query_blocks, keys, values, cache_length, id_blocks))
    return result.reshape(prompt_total * TOK_DEV, TOP, MODEL_DIMENSION)
```

```python
import functools
import math

import jax
import jax.numpy as jnp
from jax import lax
from jax.experimental import pallas as pl
from jax.experimental.pallas import tpu as pltpu
from jax.sharding import PartitionSpec as P

HEAD = 128
CAP = 2
ADAPTER_SCALE = 0.5
VMEM_LIMIT = 56 * 1024 * 1024


def attend_all(adapted_query_rows, key_block, value_block, cached):
    tok_rows, per_token, model_width = adapted_query_rows.shape
    key_total, kv_width = key_block.shape
    kv_heads = kv_width // HEAD
    group_size = model_width // kv_width
    split_query = adapted_query_rows.reshape(tok_rows, per_token, kv_heads, group_size, HEAD)
    split_keys = key_block.reshape(key_total, kv_heads, HEAD)
    split_values = value_block.reshape(key_total, kv_heads, HEAD)
    scores = jnp.einsum(
        "tagqe,jge->tagqj", split_query, split_keys, preferred_element_type=jnp.float32
    ) * (1.0 / math.sqrt(HEAD))
    key_index = lax.broadcasted_iota(jnp.int32, (tok_rows, key_total), 1)
    tok_index = lax.broadcasted_iota(jnp.int32, (tok_rows, key_total), 0)
    history = key_total - tok_rows
    visible = (key_index >= history - cached) & (key_index <= history + tok_index)
    visible = visible[:, None, None, None, :]
    scores = jnp.where(visible, scores, -1e30)
    row_peak = jnp.max(scores, axis=-1, keepdims=True)
    raised = jnp.where(visible, jnp.exp(scores - row_peak), 0.0)
    weights = (raised / jnp.sum(raised, axis=-1, keepdims=True)).astype(jnp.bfloat16)
    mixed_rows = jnp.einsum(
        "tagqj,jge->tagqe", weights, split_values, preferred_element_type=jnp.float32
    )
    return mixed_rows.reshape(tok_rows, per_token, model_width).astype(jnp.bfloat16)


def full_slots(hidden, frozen_query, keys, values, cache_length, adapter_index, down, up):
    tok_rows, model_width = hidden.shape
    per_token = adapter_index.shape[1]
    resident_count = down.shape[0]
    owners = lax.axis_size("adapt")
    flat_ids = adapter_index.reshape(-1)
    row_total = flat_ids.shape[0]
    row_index = lax.broadcasted_iota(jnp.int32, (row_total, row_total), 0)
    col_index = lax.broadcasted_iota(jnp.int32, (row_total, row_total), 1)
    matches = (flat_ids[:, None] == flat_ids[None, :]) & (col_index < row_index)
    position = flat_ids * CAP + jnp.sum(matches.astype(jnp.int32), axis=1)
    sources = jnp.broadcast_to(hidden[:, None, :], (tok_rows, per_token, model_width)).reshape(
        row_total, model_width
    )
    outgoing = (
        jnp.zeros((owners * resident_count * CAP, model_width), jnp.bfloat16)
        .at[position]
        .set(sources)
    )
    outgoing = outgoing.reshape(owners, resident_count, CAP, model_width)
    reduced_rows = jnp.einsum(
        "qtue,tve->qtuv",
        lax.all_to_all(outgoing, "adapt", split_axis=0, concat_axis=0, tiled=True),
        down,
        preferred_element_type=jnp.float32,
    ).astype(jnp.bfloat16)
    returned = lax.all_to_all(
        jnp.einsum("afok,fkx->afox", reduced_rows, up, preferred_element_type=jnp.float32).astype(
            jnp.bfloat16
        ),
        "adapt",
        split_axis=0,
        concat_axis=0,
        tiled=True,
    )
    update_rows = returned.reshape(owners * resident_count * CAP, model_width)[position]
    update_rows = update_rows.reshape(tok_rows, per_token, model_width)
    adapted_query_rows = (
        frozen_query[:, None, :].astype(jnp.float32)
        + ADAPTER_SCALE * update_rows.astype(jnp.float32)
    ).astype(jnp.bfloat16)
    return attend_all(adapted_query_rows, keys[0], values[0], cache_length[0])


def owner_kernel(folds, cap, rank, lid_ref, rows_ref, down_ref, up_ref, out_ref, part, squeezed):
    step = pl.program_id(0)
    total, width = part.shape
    block = folds * cap
    fold_of = (lax.broadcasted_iota(jnp.int32, (total, 1), 0) % block) // cap

    @pl.when(step < folds)
    def _():
        z = lax.dot_general(
            rows_ref[...],
            down_ref[...],
            (((1,), (1,)), ((), ())),
            preferred_element_type=jnp.float32,
        )
        lane = lax.broadcasted_iota(jnp.int32, (total, width), 1) // rank
        kept = jnp.where(lane == lid_ref[...], z, 0.0)
        part[...] = jnp.where(fold_of == step, kept, part[...])

    @pl.when(step == folds)
    def _():
        pairs = min(total, 16 * block)
        a = lax.broadcasted_iota(jnp.int32, (pairs, pairs), 0)
        b = lax.broadcasted_iota(jnp.int32, (pairs, pairs), 1)
        same = (a // block == b // block) & (a % cap == b % cap)
        mix = same.astype(jnp.float32)
        for start in range(0, total, pairs):
            squeezed[start : start + pairs, :] = lax.dot_general(
                mix,
                part[start : start + pairs, :],
                (((1,), (0,)), ((), ())),
                preferred_element_type=jnp.float32,
                precision=lax.Precision.HIGHEST,
            ).astype(jnp.bfloat16)

    @pl.when(step >= folds)
    def _():
        d = jnp.dot(squeezed[...], up_ref[...], preferred_element_type=jnp.float32)
        d = d.astype(jnp.bfloat16).astype(jnp.float32)
        old = out_ref[...].astype(jnp.float32)
        out_ref[...] = jnp.where(fold_of == step - folds, d, old).astype(jnp.bfloat16)


def owner_part(rows, lid, down, up, folds, cap):
    total, width = rows.shape
    resident, rank, model_width = down.shape
    ranks = resident * rank
    return pl.pallas_call(
        functools.partial(owner_kernel, folds, cap, rank),
        grid=(2 * folds,),
        in_specs=[
            pl.BlockSpec((total, 1), lambda i: (0, 0)),
            pl.BlockSpec((total, width), lambda i: (0, 0)),
            pl.BlockSpec((ranks, width), lambda i: (0, jnp.minimum(i, folds - 1))),
            pl.BlockSpec((ranks, width), lambda i: (0, jnp.maximum(i - folds, 0))),
        ],
        out_specs=pl.BlockSpec((total, width), lambda i: (0, 0)),
        out_shape=jax.ShapeDtypeStruct((total, width), jnp.bfloat16),
        scratch_shapes=[
            pltpu.VMEM((total, ranks), jnp.float32),
            pltpu.VMEM((total, ranks), jnp.bfloat16),
        ],
        compiler_params=pltpu.CompilerParams(vmem_limit_bytes=VMEM_LIMIT),
    )(lid, rows, down.reshape(ranks, model_width), up.reshape(ranks, model_width))


def attend_kernel(per_token, heads, cap, per_fold, cached_ref, pos_ref, ret_ref, frozen_ref,
                  key_ref, value_ref, out_ref, bias):
    g = pl.program_id(0)
    rows = pos_ref.shape[0]
    tokens = frozen_ref.shape[0]
    key_total = key_ref.shape[0]
    history = key_total - tokens

    @pl.when(g == 0)
    def _():
        j = lax.broadcasted_iota(jnp.int32, bias.shape, 1)
        t = (lax.broadcasted_iota(jnp.int32, bias.shape, 0) % rows) // per_token
        seen = (j >= history - cached_ref[0]) & (j <= history + t)
        bias[...] = jnp.where(seen, 0.0, -1e30)

    slots = ret_ref.shape[0]
    want = pos_ref[...] + (g // per_fold) * cap
    pick = (lax.broadcasted_iota(jnp.int32, (rows, slots), 1) == want)
    pick = pick.astype(jnp.float32).astype(jnp.bfloat16)
    update = jnp.dot(pick, ret_ref[...], preferred_element_type=jnp.float32)
    spread = (
        lax.broadcasted_iota(jnp.int32, (rows, tokens), 1)
        == lax.broadcasted_iota(jnp.int32, (rows, tokens), 0) // per_token
    )
    spread = spread.astype(jnp.float32).astype(jnp.bfloat16)
    base = jnp.dot(spread, frozen_ref[...], preferred_element_type=jnp.float32)
    query = (base + ADAPTER_SCALE * update).astype(jnp.bfloat16)
    scale = math.log2(math.e) / math.sqrt(HEAD)
    keys = key_ref[...]
    values = value_ref[...]
    for h in range(0, heads, 2):
        pair = jnp.concatenate(
            [query[:, h * HEAD : (h + 1) * HEAD], query[:, (h + 1) * HEAD : (h + 2) * HEAD]], axis=0
        )
        scores = lax.dot_general(
            pair, keys, (((1,), (1,)), ((), ())), preferred_element_type=jnp.float32
        )
        scores = scores + bias[...]
        peak = jnp.max(scores, axis=-1, keepdims=True)
        raised = jnp.exp2((scores - peak) * scale)
        whole = jnp.sum(raised, axis=-1, keepdims=True)
        mixed = jnp.dot(raised.astype(jnp.bfloat16), values, preferred_element_type=jnp.float32)
        mixed = (mixed / whole).astype(jnp.bfloat16)
        out_ref[:, h * HEAD : (h + 1) * HEAD] = mixed[:rows]
        out_ref[:, (h + 1) * HEAD : (h + 2) * HEAD] = mixed[rows:]


def attend_part(ret, pos, frozen_query, key_block, value_block, cached, per_token, cap):
    slots, width = ret.shape
    tokens, model_width = frozen_query.shape
    key_total, kv_width = key_block.shape
    kv_heads = kv_width // HEAD
    columns = model_width // kv_heads
    heads = columns // HEAD
    per_fold = width // columns
    rows = tokens * per_token
    return pl.pallas_call(
        functools.partial(attend_kernel, per_token, heads, cap, per_fold),
        grid=(kv_heads,),
        in_specs=[
            pl.BlockSpec(memory_space=pltpu.SMEM),
            pl.BlockSpec((rows, 1), lambda g: (0, 0)),
            pl.BlockSpec((slots, columns), lambda g: (0, g % per_fold)),
            pl.BlockSpec((tokens, columns), lambda g: (0, g)),
            pl.BlockSpec((key_total, HEAD), lambda g: (0, g)),
            pl.BlockSpec((key_total, HEAD), lambda g: (0, g)),
        ],
        out_specs=pl.BlockSpec((rows, columns), lambda g: (0, g)),
        out_shape=jax.ShapeDtypeStruct((rows, model_width), jnp.bfloat16),
        scratch_shapes=[pltpu.VMEM((2 * rows, key_total), jnp.float32)],
        compiler_params=pltpu.CompilerParams(vmem_limit_bytes=VMEM_LIMIT),
    )(cached, pos, ret, frozen_query, key_block, value_block)


def body(hidden, frozen_query, keys, values, cache_length, adapter_index, down, up):
    tokens, model_width = hidden.shape
    per_token = adapter_index.shape[1]
    rows = tokens * per_token
    resident = down.shape[0]
    owners = lax.axis_size("adapt")
    me = lax.axis_index("adapt")
    most = resident * CAP
    cap = most * 3 // 4 if most >= 16 else most
    folds = 16 // math.gcd(cap, 16)
    block = folds * cap
    width = model_width // folds
    slots = owners * block

    ids = adapter_index.reshape(rows)
    owner = ids // resident
    earlier = (
        lax.broadcasted_iota(jnp.int32, (rows, rows), 1)
        < lax.broadcasted_iota(jnp.int32, (rows, rows), 0)
    )
    slot = jnp.sum(((owner[:, None] == owner[None, :]) & earlier).astype(jnp.int32), axis=1)
    pos = owner * block + slot
    fits = slot < cap

    all_ids = lax.all_gather(adapter_index.reshape(1, rows), "adapt", axis=0, tiled=True)
    all_owner = all_ids // resident
    mine = all_owner == me
    rank_at = jnp.cumsum(mine.astype(jnp.int32), axis=1) - 1
    hit = mine[:, None, :] & (
        rank_at[:, None, :] == lax.broadcasted_iota(jnp.int32, (1, cap, 1), 1)
    )
    lid = jnp.sum(jnp.where(hit, all_ids[:, None, :] % resident + 1, 0), axis=2) - 1
    lid = jnp.broadcast_to(lid[:, None, :], (owners, folds, cap)).reshape(slots, 1)

    slot_index = lax.broadcasted_iota(jnp.int32, (slots, folds, tokens), 0)
    fold_index = lax.broadcasted_iota(jnp.int32, (slots, folds, tokens), 1)
    names = jnp.where(fits, pos, -1).reshape(tokens, per_token)
    pick = jnp.zeros((slots, folds, tokens), jnp.bool_)
    for k in range(per_token):
        pick = pick | (slot_index - fold_index * cap == names[:, k][None, None, :])
    pick = pick & ((slot_index % block) // cap == fold_index)
    pick = pick.astype(jnp.bfloat16).reshape(slots, folds * tokens)
    stacked = jnp.concatenate(
        [hidden[:, f * width : (f + 1) * width] for f in range(folds)], axis=0
    )
    outgoing = jnp.dot(pick, stacked, preferred_element_type=jnp.float32).astype(jnp.bfloat16)
    arrived = lax.all_to_all(
        outgoing.reshape(owners, block, width), "adapt", split_axis=0, concat_axis=0, tiled=True
    )

    def capped(arrived, lid, pos):
        delta = owner_part(arrived.reshape(slots, width), lid, down, up, folds, cap)
        returned = lax.all_to_all(
            delta.reshape(owners, block, width), "adapt", split_axis=0, concat_axis=0, tiled=True
        )
        context = attend_part(
            returned.reshape(slots, width),
            pos.reshape(rows, 1),
            frozen_query,
            keys[0],
            values[0],
            cache_length,
            per_token,
            cap,
        )
        return context.reshape(tokens, per_token, model_width)

    if cap == most:
        return capped(arrived, lid, pos)
    counts = jnp.sum(
        (
            all_owner[:, None, :]
            == lax.broadcasted_iota(jnp.int32, (1, owners, 1), 1)
        ).astype(jnp.int32),
        axis=2,
    )
    crowded = jnp.max(counts) > cap
    return lax.cond(
        crowded,
        lambda a, l, p: full_slots(
            hidden, frozen_query, keys, values, cache_length, adapter_index, down, up
        ),
        capped,
        arrived,
        lid,
        pos,
    )


def solution(mesh):
    rows2 = P(("groups", "adapt"), None)
    rows3 = P(("groups", "adapt"), None, None)
    in_specs = (rows2, rows2, rows3, rows3, P(("groups", "adapt")), rows2, rows3, rows3)
    return jax.shard_map(body, mesh=mesh, in_specs=in_specs, out_specs=rows3, check_vma=False)
```

```python
import functools
import math

import jax
import jax.numpy as jnp
from jax import lax
from jax.experimental import pallas as pl
from jax.experimental.pallas import tpu as pltpu
from jax.sharding import PartitionSpec as P

HEAD = 128
CAP = 2
ADAPTER_SCALE = 0.5
VMEM_LIMIT = 56 * 1024 * 1024


def attend_all(adapted_query_rows, key_block, value_block, cached):
    tok_rows, per_token, model_width = adapted_query_rows.shape
    key_total, kv_width = key_block.shape
    kv_heads = kv_width // HEAD
    group_size = model_width // kv_width
    split_query = adapted_query_rows.reshape(tok_rows, per_token, kv_heads, group_size, HEAD)
    split_keys = key_block.reshape(key_total, kv_heads, HEAD)
    split_values = value_block.reshape(key_total, kv_heads, HEAD)
    scores = jnp.einsum(
        "tagqe,jge->tagqj", split_query, split_keys, preferred_element_type=jnp.float32
    ) * (1.0 / math.sqrt(HEAD))
    key_index = lax.broadcasted_iota(jnp.int32, (tok_rows, key_total), 1)
    tok_index = lax.broadcasted_iota(jnp.int32, (tok_rows, key_total), 0)
    history = key_total - tok_rows
    visible = (key_index >= history - cached) & (key_index <= history + tok_index)
    visible = visible[:, None, None, None, :]
    scores = jnp.where(visible, scores, -1e30)
    row_peak = jnp.max(scores, axis=-1, keepdims=True)
    raised = jnp.where(visible, jnp.exp(scores - row_peak), 0.0)
    weights = (raised / jnp.sum(raised, axis=-1, keepdims=True)).astype(jnp.bfloat16)
    mixed_rows = jnp.einsum(
        "tagqj,jge->tagqe", weights, split_values, preferred_element_type=jnp.float32
    )
    return mixed_rows.reshape(tok_rows, per_token, model_width).astype(jnp.bfloat16)


def full_slots(hidden, frozen_query, keys, values, cache_length, adapter_index, down, up):
    tok_rows, model_width = hidden.shape
    per_token = adapter_index.shape[1]
    resident_count = down.shape[0]
    owners = lax.axis_size("adapt")
    flat_ids = adapter_index.reshape(-1)
    row_total = flat_ids.shape[0]
    row_index = lax.broadcasted_iota(jnp.int32, (row_total, row_total), 0)
    col_index = lax.broadcasted_iota(jnp.int32, (row_total, row_total), 1)
    matches = (flat_ids[:, None] == flat_ids[None, :]) & (col_index < row_index)
    position = flat_ids * CAP + jnp.sum(matches.astype(jnp.int32), axis=1)
    sources = jnp.broadcast_to(hidden[:, None, :], (tok_rows, per_token, model_width)).reshape(
        row_total, model_width
    )
    outgoing = (
        jnp.zeros((owners * resident_count * CAP, model_width), jnp.bfloat16)
        .at[position]
        .set(sources)
    )
    outgoing = outgoing.reshape(owners, resident_count, CAP, model_width)
    reduced_rows = jnp.einsum(
        "qtue,tve->qtuv",
        lax.all_to_all(outgoing, "adapt", split_axis=0, concat_axis=0, tiled=True),
        down,
        preferred_element_type=jnp.float32,
    ).astype(jnp.bfloat16)
    returned = lax.all_to_all(
        jnp.einsum("afok,fkx->afox", reduced_rows, up, preferred_element_type=jnp.float32).astype(
            jnp.bfloat16
        ),
        "adapt",
        split_axis=0,
        concat_axis=0,
        tiled=True,
    )
    update_rows = returned.reshape(owners * resident_count * CAP, model_width)[position]
    update_rows = update_rows.reshape(tok_rows, per_token, model_width)
    adapted_query_rows = (
        frozen_query[:, None, :].astype(jnp.float32)
        + ADAPTER_SCALE * update_rows.astype(jnp.float32)
    ).astype(jnp.bfloat16)
    return attend_all(adapted_query_rows, keys[0], values[0], cache_length[0])


def fold_column(total, folds, cap):
    return (lax.broadcasted_iota(jnp.int32, (total, 1), 0) % (folds * cap)) // cap


def raise_fold(fold, fold_of, squeezed_ref, up_ref, out_ref):
    d = jnp.dot(squeezed_ref[...], up_ref[...], preferred_element_type=jnp.float32)
    d = d.astype(jnp.bfloat16).astype(jnp.float32)
    old = out_ref[...].astype(jnp.float32)
    out_ref[...] = jnp.where(fold_of == fold, d, old).astype(jnp.bfloat16)


def owner_kernel(folds, cap, rank, lid_ref, rows_ref, down_ref, up_ref, out_ref, squeezed, part):
    step = pl.program_id(0)
    total, width = part.shape
    block = folds * cap
    fold_of = fold_column(total, folds, cap)

    @pl.when(step < folds)
    def _():
        z = lax.dot_general(
            rows_ref[...],
            down_ref[...],
            (((1,), (1,)), ((), ())),
            preferred_element_type=jnp.float32,
        )
        lane = lax.broadcasted_iota(jnp.int32, (total, width), 1) // rank
        kept = jnp.where(lane == lid_ref[...], z, 0.0)
        part[...] = jnp.where(fold_of == step, kept, part[...])

    @pl.when(step == folds)
    def _():
        pairs = min(total, 16 * block)
        a = lax.broadcasted_iota(jnp.int32, (pairs, pairs), 0)
        b = lax.broadcasted_iota(jnp.int32, (pairs, pairs), 1)
        same = (a // block == b // block) & (a % cap == b % cap)
        mix = same.astype(jnp.float32)
        for start in range(0, total, pairs):
            squeezed[start : start + pairs, :] = lax.dot_general(
                mix,
                part[start : start + pairs, :],
                (((1,), (0,)), ((), ())),
                preferred_element_type=jnp.float32,
                precision=lax.Precision.HIGHEST,
            ).astype(jnp.bfloat16)

    @pl.when(step >= folds)
    def _():
        raise_fold(step - folds, fold_of, squeezed, up_ref, out_ref)


def owner_part(rows, lid, down, up, folds, cap, chunks):
    total, width = rows.shape
    ranks, model_width = up.shape
    rank = ranks // (down.shape[0])
    columns = width // chunks
    return pl.pallas_call(
        functools.partial(owner_kernel, folds, cap, rank),
        grid=(2 * folds,),
        in_specs=[
            pl.BlockSpec((total, 1), lambda i: (0, 0)),
            pl.BlockSpec((total, width), lambda i: (0, 0)),
            pl.BlockSpec((ranks, width), lambda i: (0, jnp.minimum(i, folds - 1))),
            pl.BlockSpec((ranks, columns), lambda i: (0, jnp.maximum(i - folds, 0) * chunks)),
        ],
        out_specs=[
            pl.BlockSpec((total, columns), lambda i: (0, 0)),
            pl.BlockSpec((total, ranks), lambda i: (0, 0)),
        ],
        out_shape=[
            jax.ShapeDtypeStruct((total, columns), jnp.bfloat16),
            jax.ShapeDtypeStruct((total, ranks), jnp.bfloat16),
        ],
        scratch_shapes=[pltpu.VMEM((total, ranks), jnp.float32)],
        cost_estimate=pl.CostEstimate(
            flops=6 * total * ranks * model_width, bytes_accessed=40_000_000, transcendentals=0
        ),
        compiler_params=pltpu.CompilerParams(vmem_limit_bytes=VMEM_LIMIT),
    )(lid, rows, down.reshape(ranks, model_width), up)


def raise_kernel(folds, cap, squeezed_ref, up_ref, out_ref):
    fold_of = fold_column(out_ref.shape[0], folds, cap)
    raise_fold(pl.program_id(0), fold_of, squeezed_ref, up_ref, out_ref)


def raise_part(squeezed, up, folds, cap, chunks, chunk):
    total, ranks = squeezed.shape
    columns = up.shape[1] // (folds * chunks)
    return pl.pallas_call(
        functools.partial(raise_kernel, folds, cap),
        grid=(folds,),
        in_specs=[
            pl.BlockSpec((total, ranks), lambda i: (0, 0)),
            pl.BlockSpec((ranks, columns), lambda i: (0, i * chunks + chunk)),
        ],
        out_specs=pl.BlockSpec((total, columns), lambda i: (0, 0)),
        out_shape=jax.ShapeDtypeStruct((total, columns), jnp.bfloat16),
        cost_estimate=pl.CostEstimate(
            flops=2 * total * ranks * columns * folds, bytes_accessed=12_000_000, transcendentals=0
        ),
        compiler_params=pltpu.CompilerParams(vmem_limit_bytes=VMEM_LIMIT),
    )(squeezed, up)


def attend_kernel(per_token, heads, cap, cached_ref, pos_ref, ret_ref, frozen_ref, key_ref,
                  value_ref, *rest):
    out_ref, bias = rest[-2:]
    g = pl.program_id(0)
    rows = pos_ref.shape[0]
    tokens = frozen_ref.shape[0]
    key_total = key_ref.shape[0]
    history = key_total - tokens

    @pl.when(g == 0)
    def _():
        j = lax.broadcasted_iota(jnp.int32, bias.shape, 1)
        t = (lax.broadcasted_iota(jnp.int32, bias.shape, 0) % rows) // per_token
        seen = (j >= history - cached_ref[0]) & (j <= history + t)
        bias[...] = jnp.where(seen, 0.0, -1e30)

    slots = ret_ref.shape[0]
    want = pos_ref[...] + g * cap
    pick = (lax.broadcasted_iota(jnp.int32, (rows, slots), 1) == want)
    pick = pick.astype(jnp.float32).astype(jnp.bfloat16)
    update = jnp.dot(pick, ret_ref[...], preferred_element_type=jnp.float32)
    spread = (
        lax.broadcasted_iota(jnp.int32, (rows, tokens), 1)
        == lax.broadcasted_iota(jnp.int32, (rows, tokens), 0) // per_token
    )
    spread = spread.astype(jnp.float32).astype(jnp.bfloat16)
    base = jnp.dot(spread, frozen_ref[...], preferred_element_type=jnp.float32)
    query = (base + ADAPTER_SCALE * update).astype(jnp.bfloat16)
    scale = math.log2(math.e) / math.sqrt(HEAD)
    keys = key_ref[...]
    values = value_ref[...]
    for h in range(0, heads, 2):
        pair = jnp.concatenate(
            [query[:, h * HEAD : (h + 1) * HEAD], query[:, (h + 1) * HEAD : (h + 2) * HEAD]], axis=0
        )
        scores = lax.dot_general(
            pair, keys, (((1,), (1,)), ((), ())), preferred_element_type=jnp.float32
        )
        scores = scores + bias[...]
        peak = jnp.max(scores, axis=-1, keepdims=True)
        raised = jnp.exp2((scores - peak) * scale)
        whole = jnp.sum(raised, axis=-1, keepdims=True)
        mixed = jnp.dot(raised.astype(jnp.bfloat16), values, preferred_element_type=jnp.float32)
        mixed = (mixed / whole).astype(jnp.bfloat16)
        out_ref[:, h * HEAD : (h + 1) * HEAD] = mixed[:rows]
        out_ref[:, (h + 1) * HEAD : (h + 2) * HEAD] = mixed[rows:]


def attend_part(ret, pos, frozen_query, key_block, value_block, cached, per_token, cap, chunks,
                chunk, before):
    slots, columns = ret.shape
    tokens, model_width = frozen_query.shape
    key_total, kv_width = key_block.shape
    heads = columns // HEAD
    rows = tokens * per_token
    folds = model_width // (columns * chunks)
    place = lambda g: (0, g * chunks + chunk)
    operands = [cached, pos, ret, frozen_query, key_block, value_block]
    in_specs = [
        pl.BlockSpec(memory_space=pltpu.SMEM),
        pl.BlockSpec((rows, 1), lambda g: (0, 0)),
        pl.BlockSpec((slots, columns), lambda g: (0, 0)),
        pl.BlockSpec((tokens, columns), place),
        pl.BlockSpec((key_total, HEAD), place),
        pl.BlockSpec((key_total, HEAD), place),
    ]
    aliases = {}
    if before is not None:
        aliases = {len(operands): 0}
        operands.append(before)
        in_specs.append(pl.BlockSpec(memory_space=pl.ANY))
    return pl.pallas_call(
        functools.partial(attend_kernel, per_token, heads, cap),
        grid=(folds,),
        in_specs=in_specs,
        out_specs=pl.BlockSpec((rows, columns), place),
        out_shape=jax.ShapeDtypeStruct((rows, model_width), jnp.bfloat16),
        scratch_shapes=[pltpu.VMEM((2 * rows, key_total), jnp.float32)],
        input_output_aliases=aliases,
        cost_estimate=pl.CostEstimate(
            flops=4 * rows * folds * columns * key_total,
            bytes_accessed=40_000_000,
            transcendentals=rows * heads * folds * key_total,
        ),
        compiler_params=pltpu.CompilerParams(vmem_limit_bytes=VMEM_LIMIT),
    )(*operands)


def body(hidden, frozen_query, keys, values, cache_length, adapter_index, down, up):
    tokens, model_width = hidden.shape
    per_token = adapter_index.shape[1]
    rows = tokens * per_token
    resident = down.shape[0]
    owners = lax.axis_size("adapt")
    me = lax.axis_index("adapt")
    most = resident * CAP
    cap = most * 3 // 4 if most >= 16 else most
    folds = 16 // math.gcd(cap, 16)
    block = folds * cap
    width = model_width // folds
    slots = owners * block
    chunks = width // (model_width // (keys.shape[2] // HEAD))

    ids = adapter_index.reshape(rows)
    owner = ids // resident
    earlier = (
        lax.broadcasted_iota(jnp.int32, (rows, rows), 1)
        < lax.broadcasted_iota(jnp.int32, (rows, rows), 0)
    )
    slot = jnp.sum(((owner[:, None] == owner[None, :]) & earlier).astype(jnp.int32), axis=1)
    pos = owner * block + slot
    fits = slot < cap

    all_ids = lax.all_gather(adapter_index.reshape(1, rows), "adapt", axis=0, tiled=True)
    all_owner = all_ids // resident
    mine = all_owner == me
    rank_at = jnp.cumsum(mine.astype(jnp.int32), axis=1) - 1
    hit = mine[:, None, :] & (
        rank_at[:, None, :] == lax.broadcasted_iota(jnp.int32, (1, cap, 1), 1)
    )
    lid = jnp.sum(jnp.where(hit, all_ids[:, None, :] % resident + 1, 0), axis=2) - 1
    lid = jnp.broadcast_to(lid[:, None, :], (owners, folds, cap)).reshape(slots, 1)

    slot_index = lax.broadcasted_iota(jnp.int32, (slots, folds, tokens), 0)
    fold_index = lax.broadcasted_iota(jnp.int32, (slots, folds, tokens), 1)
    names = jnp.where(fits, pos, -1).reshape(tokens, per_token)
    pick = jnp.zeros((slots, folds, tokens), jnp.bool_)
    for k in range(per_token):
        pick = pick | (slot_index - fold_index * cap == names[:, k][None, None, :])
    pick = pick & ((slot_index % block) // cap == fold_index)
    pick = pick.astype(jnp.bfloat16).reshape(slots, folds * tokens)
    stacked = jnp.concatenate(
        [hidden[:, f * width : (f + 1) * width] for f in range(folds)], axis=0
    )
    outgoing = jnp.dot(pick, stacked, preferred_element_type=jnp.float32).astype(jnp.bfloat16)
    arrived = lax.all_to_all(
        outgoing.reshape(owners, block, width), "adapt", split_axis=0, concat_axis=0, tiled=True
    )

    def capped(arrived, lid, pos):
        flat_up = up.reshape(-1, model_width)
        delta, squeezed = owner_part(
            arrived.reshape(slots, width), lid, down, flat_up, folds, cap, chunks
        )
        back = []
        for chunk in range(chunks):
            if chunk:
                delta = raise_part(squeezed, flat_up, folds, cap, chunks, chunk)
            back.append(
                lax.all_to_all(
                    delta.reshape(owners, block, width // chunks),
                    "adapt",
                    split_axis=0,
                    concat_axis=0,
                    tiled=True,
                ).reshape(slots, width // chunks)
            )
        context = None
        for chunk in range(chunks):
            context = attend_part(
                back[chunk],
                pos.reshape(rows, 1),
                frozen_query,
                keys[0],
                values[0],
                cache_length,
                per_token,
                cap,
                chunks,
                chunk,
                context,
            )
        return context.reshape(tokens, per_token, model_width)

    if cap == most:
        return capped(arrived, lid, pos)
    counts = jnp.sum(
        (
            all_owner[:, None, :]
            == lax.broadcasted_iota(jnp.int32, (1, owners, 1), 1)
        ).astype(jnp.int32),
        axis=2,
    )
    crowded = jnp.max(counts) > cap
    return lax.cond(
        crowded,
        lambda a, l, p: full_slots(
            hidden, frozen_query, keys, values, cache_length, adapter_index, down, up
        ),
        capped,
        arrived,
        lid,
        pos,
    )


def solution(mesh):
    rows2 = P(("groups", "adapt"), None)
    rows3 = P(("groups", "adapt"), None, None)
    in_specs = (rows2, rows2, rows3, rows3, P(("groups", "adapt")), rows2, rows3, rows3)
    return jax.shard_map(body, mesh=mesh, in_specs=in_specs, out_specs=rows3, check_vma=False)
```

```python
import functools
import math

import jax
import jax.numpy as jnp
from jax import lax
from jax.experimental import pallas as pl
from jax.experimental.pallas import tpu as pltpu
from jax.sharding import PartitionSpec as P

HEAD = 128
CAP = 2
ADAPTER_SCALE = 0.5
VMEM_LIMIT = 56 * 1024 * 1024
TILE = 512


def attend_all(adapted_query_rows, key_block, value_block, cached):
    tok_rows, per_token, model_width = adapted_query_rows.shape
    key_total, kv_width = key_block.shape
    kv_heads = kv_width // HEAD
    group_size = model_width // kv_width
    split_query = adapted_query_rows.reshape(tok_rows, per_token, kv_heads, group_size, HEAD)
    split_keys = key_block.reshape(key_total, kv_heads, HEAD)
    split_values = value_block.reshape(key_total, kv_heads, HEAD)
    scores = jnp.einsum(
        "tagqe,jge->tagqj", split_query, split_keys, preferred_element_type=jnp.float32
    ) * (1.0 / math.sqrt(HEAD))
    key_index = lax.broadcasted_iota(jnp.int32, (tok_rows, key_total), 1)
    tok_index = lax.broadcasted_iota(jnp.int32, (tok_rows, key_total), 0)
    history = key_total - tok_rows
    visible = (key_index >= history - cached) & (key_index <= history + tok_index)
    visible = visible[:, None, None, None, :]
    scores = jnp.where(visible, scores, -1e30)
    row_peak = jnp.max(scores, axis=-1, keepdims=True)
    raised = jnp.where(visible, jnp.exp(scores - row_peak), 0.0)
    weights = (raised / jnp.sum(raised, axis=-1, keepdims=True)).astype(jnp.bfloat16)
    mixed_rows = jnp.einsum(
        "tagqj,jge->tagqe", weights, split_values, preferred_element_type=jnp.float32
    )
    return mixed_rows.reshape(tok_rows, per_token, model_width).astype(jnp.bfloat16)


def full_slots(hidden, frozen_query, keys, values, cache_length, adapter_index, down, up):
    tok_rows, model_width = hidden.shape
    per_token = adapter_index.shape[1]
    resident_count = down.shape[0]
    owners = lax.axis_size("adapt")
    flat_ids = adapter_index.reshape(-1)
    row_total = flat_ids.shape[0]
    row_index = lax.broadcasted_iota(jnp.int32, (row_total, row_total), 0)
    col_index = lax.broadcasted_iota(jnp.int32, (row_total, row_total), 1)
    matches = (flat_ids[:, None] == flat_ids[None, :]) & (col_index < row_index)
    position = flat_ids * CAP + jnp.sum(matches.astype(jnp.int32), axis=1)
    sources = jnp.broadcast_to(hidden[:, None, :], (tok_rows, per_token, model_width)).reshape(
        row_total, model_width
    )
    outgoing = (
        jnp.zeros((owners * resident_count * CAP, model_width), jnp.bfloat16)
        .at[position]
        .set(sources)
    )
    outgoing = outgoing.reshape(owners, resident_count, CAP, model_width)
    reduced_rows = jnp.einsum(
        "qtue,tve->qtuv",
        lax.all_to_all(outgoing, "adapt", split_axis=0, concat_axis=0, tiled=True),
        down,
        preferred_element_type=jnp.float32,
    ).astype(jnp.bfloat16)
    returned = lax.all_to_all(
        jnp.einsum("afok,fkx->afox", reduced_rows, up, preferred_element_type=jnp.float32).astype(
            jnp.bfloat16
        ),
        "adapt",
        split_axis=0,
        concat_axis=0,
        tiled=True,
    )
    update_rows = returned.reshape(owners * resident_count * CAP, model_width)[position]
    update_rows = update_rows.reshape(tok_rows, per_token, model_width)
    adapted_query_rows = (
        frozen_query[:, None, :].astype(jnp.float32)
        + ADAPTER_SCALE * update_rows.astype(jnp.float32)
    ).astype(jnp.bfloat16)
    return attend_all(adapted_query_rows, keys[0], values[0], cache_length[0])


def fold_column(total, folds, cap):
    return (lax.broadcasted_iota(jnp.int32, (total, 1), 0) % (folds * cap)) // cap


def raise_tile(blocked_ref, up_refs, out_ref):
    ups = jnp.concatenate([u[...] for u in up_refs], axis=0)
    d = jnp.dot(blocked_ref[...], ups, preferred_element_type=jnp.float32)
    out_ref[...] = d.astype(jnp.bfloat16)


def owner_kernel(folds, cap, rank, lid_ref, rows_ref, down_ref, *rest):
    up_refs = rest[:folds]
    out_ref, blocked, part = rest[folds:]
    step = pl.program_id(0)
    total, width = part.shape
    block = folds * cap
    fold_of = fold_column(total, folds, cap)

    @pl.when(step < folds)
    def _():
        z = lax.dot_general(
            rows_ref[...],
            down_ref[...],
            (((1,), (1,)), ((), ())),
            preferred_element_type=jnp.float32,
        )
        lane = lax.broadcasted_iota(jnp.int32, (total, width), 1) // rank
        kept = jnp.where(lane == lid_ref[...], z, 0.0)
        part[...] = jnp.where(fold_of == step, kept, part[...])

    @pl.when(step == folds)
    def _():
        pairs = min(total, 4 * block)
        a = lax.broadcasted_iota(jnp.int32, (pairs, 1), 0)
        b = lax.broadcasted_iota(jnp.int32, (1, pairs), 1)
        same = (a // block) * cap + a % cap == (b // block) * cap + b % cap
        mix = same.astype(jnp.float32)
        for start in range(0, total, pairs):
            sums = lax.dot_general(
                mix,
                part[start : start + pairs, :],
                (((1,), (0,)), ((), ())),
                preferred_element_type=jnp.float32,
                precision=lax.Precision.HIGHEST,
            )
            folded = fold_of[start : start + pairs]
            for f in range(folds):
                blocked[start : start + pairs, f * width : (f + 1) * width] = jnp.where(
                    folded == f, sums, 0.0
                ).astype(jnp.bfloat16)

    @pl.when(step >= folds)
    def _():
        raise_tile(blocked, up_refs, out_ref)


def owner_part(rows, lid, down, up, folds, cap, chunks):
    total, width = rows.shape
    ranks, model_width = up.shape
    rank = ranks // (down.shape[0])
    columns = width // chunks
    tile = min(columns, TILE)
    tiles = columns // tile
    return pl.pallas_call(
        functools.partial(owner_kernel, folds, cap, rank),
        grid=(folds + tiles,),
        in_specs=[
            pl.BlockSpec((total, 1), lambda i: (0, 0)),
            pl.BlockSpec((total, width), lambda i: (0, 0)),
            pl.BlockSpec((ranks, width), lambda i: (0, jnp.minimum(i, folds - 1))),
        ]
        + [
            pl.BlockSpec(
                (ranks, tile),
                lambda i, f=f: (0, f * chunks * tiles + jnp.maximum(i - folds, 0)),
            )
            for f in range(folds)
        ],
        out_specs=[
            pl.BlockSpec((total, tile), lambda i: (0, jnp.maximum(i - folds, 0))),
            pl.BlockSpec((total, folds * ranks), lambda i: (0, 0)),
        ],
        out_shape=[
            jax.ShapeDtypeStruct((total, columns), jnp.bfloat16),
            jax.ShapeDtypeStruct((total, folds * ranks), jnp.bfloat16),
        ],
        scratch_shapes=[pltpu.VMEM((total, ranks), jnp.float32)],
        cost_estimate=pl.CostEstimate(
            flops=6 * total * ranks * model_width, bytes_accessed=40_000_000, transcendentals=0
        ),
        compiler_params=pltpu.CompilerParams(vmem_limit_bytes=VMEM_LIMIT),
    )(lid, rows, down.reshape(ranks, model_width), *([up] * folds))


def raise_kernel(folds, blocked_ref, *rest):
    raise_tile(blocked_ref, rest[:folds], rest[folds])


def raise_part(blocked, up, folds, chunks, chunk):
    total = blocked.shape[0]
    ranks, model_width = up.shape
    columns = model_width // (folds * chunks)
    tile = min(columns, TILE)
    tiles = columns // tile
    return pl.pallas_call(
        functools.partial(raise_kernel, folds),
        grid=(tiles,),
        in_specs=[pl.BlockSpec((total, folds * ranks), lambda i: (0, 0))]
        + [
            pl.BlockSpec((ranks, tile), lambda i, f=f: (0, (f * chunks + chunk) * tiles + i))
            for f in range(folds)
        ],
        out_specs=pl.BlockSpec((total, tile), lambda i: (0, i)),
        out_shape=jax.ShapeDtypeStruct((total, columns), jnp.bfloat16),
        cost_estimate=pl.CostEstimate(
            flops=2 * total * ranks * columns * folds, bytes_accessed=12_000_000, transcendentals=0
        ),
        compiler_params=pltpu.CompilerParams(vmem_limit_bytes=VMEM_LIMIT),
    )(blocked, *([up] * folds))


def attend_kernel(per_token, heads, cap, cached_ref, pos_ref, ret_ref, frozen_ref, key_ref,
                  value_ref, *rest):
    out_ref, bias = rest[-2:]
    g = pl.program_id(0)
    rows = pos_ref.shape[0]
    tokens = frozen_ref.shape[0]
    key_total = key_ref.shape[0]
    history = key_total - tokens

    @pl.when(g == 0)
    def _():
        j = lax.broadcasted_iota(jnp.int32, bias.shape, 1)
        t = (lax.broadcasted_iota(jnp.int32, bias.shape, 0) % rows) // per_token
        seen = (j >= history - cached_ref[0]) & (j <= history + t)
        bias[...] = jnp.where(seen, 0.0, -1e30)

    slots = ret_ref.shape[0]
    want = pos_ref[...] + g * cap
    pick = (lax.broadcasted_iota(jnp.int32, (rows, slots), 1) == want)
    pick = pick.astype(jnp.float32).astype(jnp.bfloat16)
    update = jnp.dot(pick, ret_ref[...], preferred_element_type=jnp.float32)
    spread = (
        lax.broadcasted_iota(jnp.int32, (rows, tokens), 1)
        == lax.broadcasted_iota(jnp.int32, (rows, tokens), 0) // per_token
    )
    spread = spread.astype(jnp.float32).astype(jnp.bfloat16)
    base = jnp.dot(spread, frozen_ref[...], preferred_element_type=jnp.float32)
    query = (base + ADAPTER_SCALE * update).astype(jnp.bfloat16)
    scale = math.log2(math.e) / math.sqrt(HEAD)
    keys = key_ref[...]
    values = jnp.concatenate([value_ref[...], jnp.ones_like(value_ref)], axis=1)
    for h in range(0, heads, 2):
        pair = jnp.concatenate(
            [query[:, h * HEAD : (h + 1) * HEAD], query[:, (h + 1) * HEAD : (h + 2) * HEAD]], axis=0
        )
        scores = lax.dot_general(
            pair, keys, (((1,), (1,)), ((), ())), preferred_element_type=jnp.float32
        )
        scores = scores + bias[...]
        peak = jnp.max(scores, axis=-1, keepdims=True)
        raised = jnp.exp2((scores - peak) * scale)
        mixed = jnp.dot(raised.astype(jnp.bfloat16), values, preferred_element_type=jnp.float32)
        mixed = (mixed[:, :HEAD] / mixed[:, HEAD:]).astype(jnp.bfloat16)
        out_ref[:, h * HEAD : (h + 1) * HEAD] = mixed[:rows]
        out_ref[:, (h + 1) * HEAD : (h + 2) * HEAD] = mixed[rows:]


def attend_part(ret, pos, frozen_query, key_block, value_block, cached, per_token, cap, chunks,
                chunk, before):
    slots, columns = ret.shape
    tokens, model_width = frozen_query.shape
    key_total, kv_width = key_block.shape
    heads = columns // HEAD
    rows = tokens * per_token
    folds = model_width // (columns * chunks)
    place = lambda g: (0, g * chunks + chunk)
    operands = [cached, pos, ret, frozen_query, key_block, value_block]
    in_specs = [
        pl.BlockSpec(memory_space=pltpu.SMEM),
        pl.BlockSpec((rows, 1), lambda g: (0, 0)),
        pl.BlockSpec((slots, columns), lambda g: (0, 0)),
        pl.BlockSpec((tokens, columns), place),
        pl.BlockSpec((key_total, HEAD), place),
        pl.BlockSpec((key_total, HEAD), place),
    ]
    aliases = {}
    if before is not None:
        aliases = {len(operands): 0}
        operands.append(before)
        in_specs.append(pl.BlockSpec(memory_space=pl.ANY))
    return pl.pallas_call(
        functools.partial(attend_kernel, per_token, heads, cap),
        grid=(folds,),
        in_specs=in_specs,
        out_specs=pl.BlockSpec((rows, columns), place),
        out_shape=jax.ShapeDtypeStruct((rows, model_width), jnp.bfloat16),
        scratch_shapes=[pltpu.VMEM((2 * rows, key_total), jnp.float32)],
        input_output_aliases=aliases,
        cost_estimate=pl.CostEstimate(
            flops=4 * rows * folds * columns * key_total,
            bytes_accessed=40_000_000,
            transcendentals=rows * heads * folds * key_total,
        ),
        compiler_params=pltpu.CompilerParams(vmem_limit_bytes=VMEM_LIMIT),
    )(*operands)


def body(hidden, frozen_query, keys, values, cache_length, adapter_index, down, up):
    tokens, model_width = hidden.shape
    per_token = adapter_index.shape[1]
    rows = tokens * per_token
    resident = down.shape[0]
    owners = lax.axis_size("adapt")
    me = lax.axis_index("adapt")
    most = resident * CAP
    cap = most * 3 // 4 if most >= 16 else most
    folds = 16 // math.gcd(cap, 16)
    block = folds * cap
    width = model_width // folds
    slots = owners * block
    chunks = width // (model_width // (keys.shape[2] // HEAD))

    ids = adapter_index.reshape(rows)
    owner = ids // resident
    earlier = (
        lax.broadcasted_iota(jnp.int32, (rows, rows), 1)
        < lax.broadcasted_iota(jnp.int32, (rows, rows), 0)
    )
    slot = jnp.sum(((owner[:, None] == owner[None, :]) & earlier).astype(jnp.int32), axis=1)
    pos = owner * block + slot
    fits = slot < cap

    all_ids = lax.all_gather(adapter_index.reshape(1, rows), "adapt", axis=0, tiled=True)
    all_owner = all_ids // resident
    mine = all_owner == me
    rank_at = jnp.cumsum(mine.astype(jnp.int32), axis=1) - 1
    hit = mine[:, None, :] & (
        rank_at[:, None, :] == lax.broadcasted_iota(jnp.int32, (1, cap, 1), 1)
    )
    lid = jnp.sum(jnp.where(hit, all_ids[:, None, :] % resident + 1, 0), axis=2) - 1
    lid = jnp.broadcast_to(lid[:, None, :], (owners, folds, cap)).reshape(slots, 1)

    slot_index = lax.broadcasted_iota(jnp.int32, (slots, folds, tokens), 0)
    fold_index = lax.broadcasted_iota(jnp.int32, (slots, folds, tokens), 1)
    names = jnp.where(fits, pos, -1).reshape(tokens, per_token)
    pick = jnp.zeros((slots, folds, tokens), jnp.bool_)
    for k in range(per_token):
        pick = pick | (slot_index - fold_index * cap == names[:, k][None, None, :])
    pick = pick & ((slot_index % block) // cap == fold_index)
    pick = pick.astype(jnp.bfloat16).reshape(slots, folds * tokens)
    stacked = jnp.concatenate(
        [hidden[:, f * width : (f + 1) * width] for f in range(folds)], axis=0
    )
    outgoing = jnp.dot(pick, stacked, preferred_element_type=jnp.float32).astype(jnp.bfloat16)
    arrived = lax.all_to_all(
        outgoing.reshape(owners, block, width), "adapt", split_axis=0, concat_axis=0, tiled=True
    )

    def capped(arrived, lid, pos):
        flat_up = up.reshape(-1, model_width)
        delta, squeezed = owner_part(
            arrived.reshape(slots, width), lid, down, flat_up, folds, cap, chunks
        )
        back = []
        for chunk in range(chunks):
            if chunk:
                delta = raise_part(squeezed, flat_up, folds, chunks, chunk)
            back.append(
                lax.all_to_all(
                    delta.reshape(owners, block, width // chunks),
                    "adapt",
                    split_axis=0,
                    concat_axis=0,
                    tiled=True,
                ).reshape(slots, width // chunks)
            )
        context = None
        for chunk in range(chunks):
            context = attend_part(
                back[chunk],
                pos.reshape(rows, 1),
                frozen_query,
                keys[0],
                values[0],
                cache_length,
                per_token,
                cap,
                chunks,
                chunk,
                context,
            )
        return context.reshape(tokens, per_token, model_width)

    if cap == most:
        return capped(arrived, lid, pos)
    counts = jnp.sum(
        (
            all_owner[:, None, :]
            == lax.broadcasted_iota(jnp.int32, (1, owners, 1), 1)
        ).astype(jnp.int32),
        axis=2,
    )
    crowded = jnp.max(counts) > cap
    return lax.cond(
        crowded,
        lambda a, l, p: full_slots(
            hidden, frozen_query, keys, values, cache_length, adapter_index, down, up
        ),
        capped,
        arrived,
        lid,
        pos,
    )


def solution(mesh):
    rows2 = P(("groups", "adapt"), None)
    rows3 = P(("groups", "adapt"), None, None)
    in_specs = (rows2, rows2, rows3, rows3, P(("groups", "adapt")), rows2, rows3, rows3)
    return jax.shard_map(body, mesh=mesh, in_specs=in_specs, out_specs=rows3, check_vma=False)
```

```python
import functools
import math

import jax
import jax.numpy as jnp
from jax import lax
from jax.experimental import pallas as pl
from jax.experimental.pallas import tpu as pltpu
from jax.sharding import PartitionSpec as P

HEAD = 128
CAP = 2
ADAPTER_SCALE = 0.5
VMEM_LIMIT = 56 * 1024 * 1024
TILE = 512


def attend_all(adapted_query_rows, key_block, value_block, cached):
    tok_rows, per_token, model_width = adapted_query_rows.shape
    key_total, kv_width = key_block.shape
    kv_heads = kv_width // HEAD
    group_size = model_width // kv_width
    split_query = adapted_query_rows.reshape(tok_rows, per_token, kv_heads, group_size, HEAD)
    split_keys = key_block.reshape(key_total, kv_heads, HEAD)
    split_values = value_block.reshape(key_total, kv_heads, HEAD)
    scores = jnp.einsum(
        "tagqe,jge->tagqj", split_query, split_keys, preferred_element_type=jnp.float32
    ) * (1.0 / math.sqrt(HEAD))
    key_index = lax.broadcasted_iota(jnp.int32, (tok_rows, key_total), 1)
    tok_index = lax.broadcasted_iota(jnp.int32, (tok_rows, key_total), 0)
    history = key_total - tok_rows
    visible = (key_index >= history - cached) & (key_index <= history + tok_index)
    visible = visible[:, None, None, None, :]
    scores = jnp.where(visible, scores, -1e30)
    row_peak = jnp.max(scores, axis=-1, keepdims=True)
    raised = jnp.where(visible, jnp.exp(scores - row_peak), 0.0)
    weights = (raised / jnp.sum(raised, axis=-1, keepdims=True)).astype(jnp.bfloat16)
    mixed_rows = jnp.einsum(
        "tagqj,jge->tagqe", weights, split_values, preferred_element_type=jnp.float32
    )
    return mixed_rows.reshape(tok_rows, per_token, model_width).astype(jnp.bfloat16)


def full_slots(hidden, frozen_query, keys, values, cache_length, adapter_index, down, up):
    tok_rows, model_width = hidden.shape
    per_token = adapter_index.shape[1]
    resident_count = down.shape[0]
    owners = lax.axis_size("adapt")
    flat_ids = adapter_index.reshape(-1)
    row_total = flat_ids.shape[0]
    row_index = lax.broadcasted_iota(jnp.int32, (row_total, row_total), 0)
    col_index = lax.broadcasted_iota(jnp.int32, (row_total, row_total), 1)
    matches = (flat_ids[:, None] == flat_ids[None, :]) & (col_index < row_index)
    position = flat_ids * CAP + jnp.sum(matches.astype(jnp.int32), axis=1)
    sources = jnp.broadcast_to(hidden[:, None, :], (tok_rows, per_token, model_width)).reshape(
        row_total, model_width
    )
    outgoing = (
        jnp.zeros((owners * resident_count * CAP, model_width), jnp.bfloat16)
        .at[position]
        .set(sources)
    )
    outgoing = outgoing.reshape(owners, resident_count, CAP, model_width)
    reduced_rows = jnp.einsum(
        "qtue,tve->qtuv",
        lax.all_to_all(outgoing, "adapt", split_axis=0, concat_axis=0, tiled=True),
        down,
        preferred_element_type=jnp.float32,
    ).astype(jnp.bfloat16)
    returned = lax.all_to_all(
        jnp.einsum("afok,fkx->afox", reduced_rows, up, preferred_element_type=jnp.float32).astype(
            jnp.bfloat16
        ),
        "adapt",
        split_axis=0,
        concat_axis=0,
        tiled=True,
    )
    update_rows = returned.reshape(owners * resident_count * CAP, model_width)[position]
    update_rows = update_rows.reshape(tok_rows, per_token, model_width)
    adapted_query_rows = (
        frozen_query[:, None, :].astype(jnp.float32)
        + ADAPTER_SCALE * update_rows.astype(jnp.float32)
    ).astype(jnp.bfloat16)
    return attend_all(adapted_query_rows, keys[0], values[0], cache_length[0])


def fold_column(total, folds, cap):
    return (lax.broadcasted_iota(jnp.int32, (total, 1), 0) % (folds * cap)) // cap


def raise_tile(blocked_ref, up_refs, out_ref):
    ups = jnp.concatenate([u[...] for u in up_refs], axis=0)
    d = jnp.dot(blocked_ref[...], ups, preferred_element_type=jnp.float32)
    out_ref[...] = d.astype(jnp.bfloat16)


def owner_kernel(folds, cap, rank, lid_ref, rows_ref, down_ref, *rest):
    up_refs = rest[:folds]
    out_ref, blocked, part = rest[folds:]
    step = pl.program_id(0)
    total, width = part.shape
    block = folds * cap
    fold_of = fold_column(total, folds, cap)

    @pl.when(step < folds)
    def _():
        z = lax.dot_general(
            rows_ref[...],
            down_ref[...],
            (((1,), (1,)), ((), ())),
            preferred_element_type=jnp.float32,
        )
        lane = lax.broadcasted_iota(jnp.int32, (total, width), 1) // rank
        kept = jnp.where(lane == lid_ref[...], z, 0.0)
        part[...] = jnp.where(fold_of == step, kept, part[...])

    @pl.when(step == folds)
    def _():
        pairs = min(total, 4 * block)
        a = lax.broadcasted_iota(jnp.int32, (pairs, 1), 0)
        b = lax.broadcasted_iota(jnp.int32, (1, pairs), 1)
        same = (a // block) * cap + a % cap == (b // block) * cap + b % cap
        mix = same.astype(jnp.float32)
        for start in range(0, total, pairs):
            sums = lax.dot_general(
                mix,
                part[start : start + pairs, :],
                (((1,), (0,)), ((), ())),
                preferred_element_type=jnp.float32,
                precision=lax.Precision.HIGHEST,
            )
            folded = fold_of[start : start + pairs]
            for f in range(folds):
                blocked[start : start + pairs, f * width : (f + 1) * width] = jnp.where(
                    folded == f, sums, 0.0
                ).astype(jnp.bfloat16)

    @pl.when(step >= folds)
    def _():
        raise_tile(blocked, up_refs, out_ref)


def owner_part(rows, lid, down, up, folds, cap, chunks):
    total, width = rows.shape
    ranks, model_width = up.shape
    rank = ranks // (down.shape[0])
    columns = width // chunks
    tile = min(columns, TILE)
    tiles = columns // tile
    return pl.pallas_call(
        functools.partial(owner_kernel, folds, cap, rank),
        grid=(folds + tiles,),
        in_specs=[
            pl.BlockSpec((total, 1), lambda i: (0, 0)),
            pl.BlockSpec((total, width), lambda i: (0, 0)),
            pl.BlockSpec((ranks, width), lambda i: (0, jnp.minimum(i, folds - 1))),
        ]
        + [
            pl.BlockSpec(
                (ranks, tile),
                lambda i, f=f: (0, f * chunks * tiles + jnp.maximum(i - folds, 0)),
            )
            for f in range(folds)
        ],
        out_specs=[
            pl.BlockSpec((total, tile), lambda i: (0, jnp.maximum(i - folds, 0))),
            pl.BlockSpec((total, folds * ranks), lambda i: (0, 0)),
        ],
        out_shape=[
            jax.ShapeDtypeStruct((total, columns), jnp.bfloat16),
            jax.ShapeDtypeStruct((total, folds * ranks), jnp.bfloat16),
        ],
        scratch_shapes=[pltpu.VMEM((total, ranks), jnp.float32)],
        cost_estimate=pl.CostEstimate(
            flops=6 * total * ranks * model_width, bytes_accessed=40_000_000, transcendentals=0
        ),
        compiler_params=pltpu.CompilerParams(vmem_limit_bytes=VMEM_LIMIT),
    )(lid, rows, down.reshape(ranks, model_width), *([up] * folds))


def raise_kernel(folds, blocked_ref, *rest):
    raise_tile(blocked_ref, rest[:folds], rest[folds])


def raise_part(blocked, up, folds, chunks, chunk):
    total = blocked.shape[0]
    ranks, model_width = up.shape
    columns = model_width // (folds * chunks)
    tile = min(columns, TILE)
    tiles = columns // tile
    return pl.pallas_call(
        functools.partial(raise_kernel, folds),
        grid=(tiles,),
        in_specs=[pl.BlockSpec((total, folds * ranks), lambda i: (0, 0))]
        + [
            pl.BlockSpec((ranks, tile), lambda i, f=f: (0, (f * chunks + chunk) * tiles + i))
            for f in range(folds)
        ],
        out_specs=pl.BlockSpec((total, tile), lambda i: (0, i)),
        out_shape=jax.ShapeDtypeStruct((total, columns), jnp.bfloat16),
        cost_estimate=pl.CostEstimate(
            flops=2 * total * ranks * columns * folds, bytes_accessed=12_000_000, transcendentals=0
        ),
        compiler_params=pltpu.CompilerParams(vmem_limit_bytes=VMEM_LIMIT),
    )(blocked, *([up] * folds))


def attend_kernel(per_token, heads, cap, cached_ref, pos_ref, ret_ref, frozen_ref, key_ref,
                  value_ref, *rest):
    out_ref, bias = rest[-2:]
    g = pl.program_id(0)
    rows = pos_ref.shape[0]
    tokens = frozen_ref.shape[0]
    key_total = key_ref.shape[0]
    history = key_total - tokens

    @pl.when(g == 0)
    def _():
        j = lax.broadcasted_iota(jnp.int32, bias.shape, 1)
        t = (lax.broadcasted_iota(jnp.int32, bias.shape, 0) % rows) // per_token
        seen = (j >= history - cached_ref[0]) & (j <= history + t)
        bias[...] = jnp.where(seen, 0.0, -1e30)

    slots = ret_ref.shape[0]
    want = pos_ref[...] + g * cap
    pick = (lax.broadcasted_iota(jnp.int32, (rows, slots), 1) == want)
    pick = pick.astype(jnp.float32).astype(jnp.bfloat16)
    update = jnp.dot(pick, ret_ref[...], preferred_element_type=jnp.float32)
    spread = (
        lax.broadcasted_iota(jnp.int32, (rows, tokens), 1)
        == lax.broadcasted_iota(jnp.int32, (rows, tokens), 0) // per_token
    )
    spread = spread.astype(jnp.float32).astype(jnp.bfloat16)
    base = jnp.dot(spread, frozen_ref[...], preferred_element_type=jnp.float32)
    query = (base + ADAPTER_SCALE * update).astype(jnp.bfloat16)
    scale = math.log2(math.e) / math.sqrt(HEAD)
    keys = key_ref[...]
    values = jnp.concatenate([value_ref[...], jnp.ones_like(value_ref)], axis=1)
    for h in range(0, heads, 2):
        pair = jnp.concatenate(
            [query[:, h * HEAD : (h + 1) * HEAD], query[:, (h + 1) * HEAD : (h + 2) * HEAD]], axis=0
        )
        scores = lax.dot_general(
            pair, keys, (((1,), (1,)), ((), ())), preferred_element_type=jnp.float32
        )
        scores = scores + bias[...]
        peak = jnp.max(scores, axis=-1, keepdims=True)
        raised = jnp.exp2((scores - peak) * scale)
        mixed = jnp.dot(raised.astype(jnp.bfloat16), values, preferred_element_type=jnp.float32)
        mixed = mixed[:, :HEAD] / mixed[:, HEAD:]
        mixed = mixed.reshape(2 * tokens, per_token, HEAD).astype(jnp.bfloat16)
        out_ref[:, :, h * HEAD : (h + 1) * HEAD] = mixed[:tokens]
        out_ref[:, :, (h + 1) * HEAD : (h + 2) * HEAD] = mixed[tokens:]


def attend_part(ret, pos, frozen_query, key_block, value_block, cached, per_token, cap, chunks,
                chunk, before):
    slots, columns = ret.shape
    tokens, model_width = frozen_query.shape
    key_total, kv_width = key_block.shape
    heads = columns // HEAD
    rows = tokens * per_token
    folds = model_width // (columns * chunks)
    place = lambda g: (0, g * chunks + chunk)
    operands = [cached, pos, ret, frozen_query, key_block, value_block]
    in_specs = [
        pl.BlockSpec(memory_space=pltpu.SMEM),
        pl.BlockSpec((rows, 1), lambda g: (0, 0)),
        pl.BlockSpec((slots, columns), lambda g: (0, 0)),
        pl.BlockSpec((tokens, columns), place),
        pl.BlockSpec((key_total, HEAD), place),
        pl.BlockSpec((key_total, HEAD), place),
    ]
    aliases = {}
    if before is not None:
        aliases = {len(operands): 0}
        operands.append(before)
        in_specs.append(pl.BlockSpec(memory_space=pl.ANY))
    return pl.pallas_call(
        functools.partial(attend_kernel, per_token, heads, cap),
        grid=(folds,),
        in_specs=in_specs,
        out_specs=pl.BlockSpec((tokens, per_token, columns), lambda g: (0, 0, g * chunks + chunk)),
        out_shape=jax.ShapeDtypeStruct((tokens, per_token, model_width), jnp.bfloat16),
        scratch_shapes=[pltpu.VMEM((2 * rows, key_total), jnp.float32)],
        input_output_aliases=aliases,
        cost_estimate=pl.CostEstimate(
            flops=4 * rows * folds * columns * key_total,
            bytes_accessed=40_000_000,
            transcendentals=rows * heads * folds * key_total,
        ),
        compiler_params=pltpu.CompilerParams(vmem_limit_bytes=VMEM_LIMIT),
    )(*operands)


def body(hidden, frozen_query, keys, values, cache_length, adapter_index, down, up):
    tokens, model_width = hidden.shape
    per_token = adapter_index.shape[1]
    rows = tokens * per_token
    resident = down.shape[0]
    owners = lax.axis_size("adapt")
    me = lax.axis_index("adapt")
    most = resident * CAP
    cap = most * 3 // 4 if most >= 16 else most
    folds = 16 // math.gcd(cap, 16)
    block = folds * cap
    width = model_width // folds
    slots = owners * block
    chunks = width // (model_width // (keys.shape[2] // HEAD))

    ids = adapter_index.reshape(rows)
    owner = ids // resident
    earlier = (
        lax.broadcasted_iota(jnp.int32, (rows, rows), 1)
        < lax.broadcasted_iota(jnp.int32, (rows, rows), 0)
    )
    slot = jnp.sum(((owner[:, None] == owner[None, :]) & earlier).astype(jnp.int32), axis=1)
    pos = owner * block + slot
    fits = slot < cap

    all_ids = lax.all_gather(adapter_index.reshape(1, rows), "adapt", axis=0, tiled=True)
    all_owner = all_ids // resident
    mine = all_owner == me
    rank_at = jnp.cumsum(mine.astype(jnp.int32), axis=1) - 1
    hit = mine[:, None, :] & (
        rank_at[:, None, :] == lax.broadcasted_iota(jnp.int32, (1, cap, 1), 1)
    )
    lid = jnp.sum(jnp.where(hit, all_ids[:, None, :] % resident + 1, 0), axis=2) - 1
    lid = jnp.broadcast_to(lid[:, None, :], (owners, folds, cap)).reshape(slots, 1)

    slot_index = lax.broadcasted_iota(jnp.int32, (slots, folds, tokens), 0)
    fold_index = lax.broadcasted_iota(jnp.int32, (slots, folds, tokens), 1)
    names = jnp.where(fits, pos, -1).reshape(tokens, per_token)
    pick = jnp.zeros((slots, folds, tokens), jnp.bool_)
    for k in range(per_token):
        pick = pick | (slot_index - fold_index * cap == names[:, k][None, None, :])
    pick = pick & ((slot_index % block) // cap == fold_index)
    pick = pick.astype(jnp.bfloat16).reshape(slots, folds * tokens)
    stacked = jnp.concatenate(
        [hidden[:, f * width : (f + 1) * width] for f in range(folds)], axis=0
    )
    outgoing = jnp.dot(pick, stacked, preferred_element_type=jnp.float32).astype(jnp.bfloat16)
    arrived = lax.all_to_all(
        outgoing.reshape(owners, block, width), "adapt", split_axis=0, concat_axis=0, tiled=True
    )

    def capped(arrived, lid, pos):
        flat_up = up.reshape(-1, model_width)
        delta, squeezed = owner_part(
            arrived.reshape(slots, width), lid, down, flat_up, folds, cap, chunks
        )
        back = []
        for chunk in range(chunks):
            if chunk:
                delta = raise_part(squeezed, flat_up, folds, chunks, chunk)
            back.append(
                lax.all_to_all(
                    delta.reshape(owners, block, width // chunks),
                    "adapt",
                    split_axis=0,
                    concat_axis=0,
                    tiled=True,
                ).reshape(slots, width // chunks)
            )
        context = None
        for chunk in range(chunks):
            context = attend_part(
                back[chunk],
                pos.reshape(rows, 1),
                frozen_query,
                keys[0],
                values[0],
                cache_length,
                per_token,
                cap,
                chunks,
                chunk,
                context,
            )
        return context

    if cap == most:
        return capped(arrived, lid, pos)
    counts = jnp.sum(
        (
            all_owner[:, None, :]
            == lax.broadcasted_iota(jnp.int32, (1, owners, 1), 1)
        ).astype(jnp.int32),
        axis=2,
    )
    crowded = jnp.max(counts) > cap
    return lax.cond(
        crowded,
        lambda a, l, p: full_slots(
            hidden, frozen_query, keys, values, cache_length, adapter_index, down, up
        ),
        capped,
        arrived,
        lid,
        pos,
    )


def solution(mesh):
    rows2 = P(("groups", "adapt"), None)
    rows3 = P(("groups", "adapt"), None, None)
    in_specs = (rows2, rows2, rows3, rows3, P(("groups", "adapt")), rows2, rows3, rows3)
    return jax.shard_map(body, mesh=mesh, in_specs=in_specs, out_specs=rows3, check_vma=False)
```
